128 devices in a mesh: rows: 128 (over y, x, z, core).
Axes of the slice: x: 4, y: 4, z: 4, core: 2. Of those that a mesh axis runs over, the one named last changes fastest.
Arguments:
- hologram: float32 [2, 65536, 1024], P(None, 'rows'), may hold values from -6 to 6
- phase: float32 [32768, 1024], P('rows'), may hold values from -3.140625 to 3.140625
- kept_blocks: int32 [512], replicated, may hold values from 0 to 1023, as said below
Outputs:
- propagated: float32 [2, 32768, 1024], P(None, 'rows')
The draws below stay inside these ranges and needn't reach their ends.
Inputs may be any that keep to these rules, and one draw needn't show every extreme that they name: `kept_blocks`: distinct block indices; blocks 0 and 1023 are always kept.
All inputs are finite; a program needn't handle non-finite values.
Results may differ from the reference program's by a relative error of at most 0.00013.
Values sent between devices are 32-bit elements; how exact they have to be, the bound alone decides.
A program may use at most 64 MiB of HBM per device.

```python
import math
import jax
import jax.numpy as jnp
from jax import lax

N = 65536
W = 1024
BLK = 64
K = 512


def draw_kept_blocks(key, part):
    key = jax.random.fold_in(key, 7)
    first_key, second_key = jax.random.split(key)
    inner = jax.random.permutation(first_key, N // BLK - 2).astype(jnp.int32) + 1
    chosen = jnp.concatenate([jnp.array([0, N // BLK - 1], jnp.int32), inner[:K - 2]])
    return jax.random.permutation(second_key, chosen).astype(jnp.int32)


def block_levels(stream_key, extent, cuts, least, high):
    level = 1.0
    for position, parts in cuts:
        heights = jax.random.uniform(jax.random.fold_in(jax.random.fold_in(stream_key, 6), position), (parts,), jnp.float32, least / len(cuts), high / len(cuts))
        level = level * jnp.repeat(jnp.exp(heights), extent[position] // parts).reshape((-1,) + (1,) * (len(extent) - 1 - position))
    return level


def bell_draw(own_key, dims, width, reach, shards=(), held_as=jnp.bfloat16):
    values = width * jax.random.normal(own_key, dims, jnp.float32)
    if shards:
        values = values * block_levels(own_key, dims, shards, -0.22, 0.18)
    return jnp.clip(values, -reach, reach).astype(held_as)


def setup_inputs(seed: int = 0) -> dict:
    arg_keys = jax.random.split(jax.random.key(seed), 4)
    hologram = bell_draw(arg_keys[0], (2, N, W), 1.0, 6.0, ((1, 128),), jnp.float32)
    phase = jnp.clip(jax.random.uniform(arg_keys[1], (K * BLK, W), jnp.float32, -3.140625, 3.140625), -3.140625, 3.140625)
    kept_blocks = draw_kept_blocks(jax.random.fold_in(arg_keys[3], 71), 0)
    return dict(hologram=hologram, phase=phase, kept_blocks=kept_blocks)


def reference(hologram, phase, kept_blocks):
    signal = lax.complex(hologram[0], hologram[1])
    spectrum = jnp.fft.fft(signal, axis=0) * (1.0 / math.sqrt(N))
    offsets = jnp.arange(BLK, dtype=jnp.int32)
    row_ids = (kept_blocks[:, None] * BLK + offsets[None, :]).reshape(-1).astype(jnp.int32)
    selected = spectrum[row_ids]
    rotated = selected * lax.complex(jnp.cos(phase), jnp.sin(phase))
    return jnp.stack([jnp.real(rotated), jnp.imag(rotated)]).astype(jnp.float32)
```

```python
import jax
import jax.numpy as jnp
import numpy as np
from jax import lax
from jax.experimental import pallas as pl
from jax.experimental.pallas import tpu as pltpu
from jax.sharding import PartitionSpec as P

MESH = pl.DeviceIdType.MESH
DEVS = 128
ROWS = 512
COLS = 1024
HALVES = 2
CPC = 4
RAD = 256
SPEC = 512 * 8
STEP = 37


def tables():
    def split(a):
        a = a.astype(np.float32)
        hi = a.astype(jnp.bfloat16)
        lo = (a - hi.astype(np.float32)).astype(jnp.bfloat16)
        return hi, lo

    def real_form(angle):
        cos, sin = np.cos(angle), np.sin(angle)
        return np.block([[cos, sin], [-sin, cos]])

    k = np.arange(RAD)
    m = np.concatenate([2 * np.arange(DEVS), 2 * np.arange(DEVS) + 1])
    first = real_form(2 * np.pi * (np.outer(k, m) % RAD) / RAD)
    second = real_form(2 * np.pi * (np.outer(k, k) % RAD) / RAD)
    out = []
    for mat in (first, second):
        hi, lo = split(mat)
        out.append(np.concatenate([hi, hi, lo], axis=1))
    angle = 2 * np.pi * np.outer(k, k) / (RAD * RAD)
    twiddle = np.stack([np.cos(angle), np.sin(angle)]) / RAD
    return out[0], out[1], twiddle.astype(np.float32)


def peer_of(me, i):
    i = lax.rem(i * STEP, DEVS)
    core = lax.rem(me + i, 2)
    z = lax.rem(lax.div(me, 2) + lax.div(i, 2), 4)
    x = lax.rem(lax.div(me, 8) + lax.div(i, 8), 4)
    y = lax.rem(lax.div(me, 32) + lax.div(i, 32), 4)
    return ((y * 4 + x) * 4 + z) * 2 + core


def split3(a, axis):
    hi = a.astype(jnp.bfloat16)
    lo = (a - hi.astype(jnp.float32)).astype(jnp.bfloat16)
    return jnp.concatenate([hi, lo, hi], axis=axis)


def aligned(v, m):
    return pl.multiple_of(v, m)


def kernel(
    x_hbm, phase_hbm, g1_hbm, g2_hbm, tw_hbm, kept, out_hbm,
    x_v, s_in, r_in, spec, s_out, r_out, cos_v, sin_v, g1, g2, tw, out_v,
    x_sem, t_sem, o_sem, ss_in, rs_in, ss_out, rs_out,
):
    me = lax.axis_index("rows")
    barrier = pltpu.get_barrier_semaphore()

    def greet(i, c):
        pl.semaphore_signal(
            barrier, inc=1, device_id=(peer_of(me, i),), device_id_type=MESH
        )
        return c

    lax.fori_loop(1, DEVS, greet, 0)

    x_copies = [
        pltpu.make_async_copy(
            x_hbm.at[:, :, pl.ds(h * 512, 512)], x_v.at[h], x_sem.at[h]
        )
        for h in range(HALVES)
    ]
    for copy in x_copies:
        copy.start()
    table_copies = [
        pltpu.make_async_copy(src, dst, t_sem.at[n])
        for n, (src, dst) in enumerate(
            [(phase_hbm, cos_v), (g1_hbm, g1), (g2_hbm, g2), (tw_hbm, tw)]
        )
    ]
    for copy in table_copies:
        copy.start()

    def prepare(h):
        x_copies[h].wait()
        for ri in range(2):

            def one(c4, c):
                block = x_v[h, ri, :, pl.ds(aligned(c4 * 128, 128), 128)].T
                for rq in range(4):
                    s_in[h, pl.ds(rq * 8 + ri * 4 + c4, DEVS, stride=32), :] = block[
                        :, rq * 128 : (rq + 1) * 128
                    ]
                return c

            lax.fori_loop(0, CPC, one, 0)

    def send_in(h):
        def one(i, c):
            p = peer_of(me, i)
            pltpu.make_async_remote_copy(
                src_ref=s_in.at[h, pl.ds(aligned(p * 32, 32), 32)],
                dst_ref=r_in.at[h, pl.ds(aligned(me * 32, 32), 32)],
                send_sem=ss_in.at[h],
                recv_sem=rs_in.at[h],
                device_id=(p,),
                device_id_type=MESH,
            ).start()
            return c

        lax.fori_loop(1, DEVS, one, 0)
        own = pl.ds(aligned(me * 32, 32), 32)
        r_in[h, own, :] = s_in[h, own, :]

    def wait_bytes(ref, sem, h, rows):
        part = ref.at[h, pl.ds(0, rows)]
        pltpu.make_async_copy(part, part, sem.at[h]).wait()

    prepare(0)
    pl.semaphore_wait(barrier, DEVS - 1)
    send_in(0)
    prepare(1)
    send_in(1)

    table_copies[0].wait()

    def trig(i, c):
        rows = pl.ds(aligned(i * 8, 8), 8)
        angle = cos_v[rows, :]
        cos_v[rows, :] = jnp.cos(angle)
        sin_v[rows, :] = jnp.sin(angle)
        return c

    lax.fori_loop(0, 32, trig, 0)
    for copy in table_copies[1:]:
        copy.wait()

    flat = spec.reshape(2 * SPEC, 128)

    def transform(h):
        def one(c4, c):
            parts = []
            for ri in range(2):
                for rh in range(2):
                    parts.append(
                        jnp.concatenate(
                            [
                                r_in[
                                    h,
                                    pl.ds(
                                        (rh * 2 + rl) * 8 + ri * 4 + c4,
                                        DEVS,
                                        stride=32,
                                    ),
                                    :,
                                ]
                                for rl in range(2)
                            ],
                            axis=1,
                        )
                    )
            a = split3(jnp.concatenate(parts, axis=0), 0)
            y = jnp.dot(g1[...], a, preferred_element_type=jnp.float32)
            y_re, y_im = y[:RAD], y[RAD:]
            t_re, t_im = tw[0], tw[1]
            b = jnp.concatenate(
                [y_re * t_re + y_im * t_im, y_im * t_re - y_re * t_im], axis=1
            )
            z = lax.dot_general(
                g2[...],
                split3(b, 1),
                (((1,), (1,)), ((), ())),
                preferred_element_type=jnp.float32,
            )
            for ro in range(2):
                for kh in range(2):
                    tile = z[ro * RAD : (ro + 1) * RAD, kh * 128 : (kh + 1) * 128]
                    swapped = jnp.concatenate([tile[:, 64:], tile[:, :64]], axis=1)
                    row = kh * 8 + ro * 4 + c4
                    flat[pl.ds(row, RAD, stride=16), :] = tile
                    flat[pl.ds(SPEC + row, RAD, stride=16), :] = swapped
            return c

        lax.fori_loop(0, CPC, one, 0)

    low = lax.broadcasted_iota(jnp.int32, (8, 128), 1) < 64

    def gather(p):
        tiles = []
        for jp in range(2):
            halves = []
            for par in range(2):
                b = kept[p * 4 + jp * 2 + par]
                halves.append(spec[lax.div(b, 2) + lax.rem(b + par, 2) * 512])
            tiles.append(jnp.where(low, halves[0], halves[1]))
        return jnp.concatenate(tiles, axis=0)

    def send_out(h):
        def one(i, c):
            p = peer_of(me, i)
            mine = pl.ds(aligned(p * 16, 16), 16)
            s_out[h, mine, :] = gather(p)
            pltpu.make_async_remote_copy(
                src_ref=s_out.at[h, mine],
                dst_ref=r_out.at[h, pl.ds(aligned(me * 16, 16), 16)],
                send_sem=ss_out.at[h],
                recv_sem=rs_out.at[h],
                device_id=(p,),
                device_id_type=MESH,
            ).start()
            return c

        lax.fori_loop(1, DEVS, one, 0)
        r_out[h, pl.ds(aligned(me * 16, 16), 16), :] = gather(me)

    def finish(h):
        def one(c4, c):
            lanes = pl.ds(aligned((h * CPC + c4) * 128, 128), 128)
            for jp in range(2):
                rows = pl.ds(jp * 128, 128)
                re, im = [
                    r_out[h, pl.ds(jp * 8 + ri * 4 + c4, DEVS, stride=16), :].T
                    for ri in range(2)
                ]
                cos, sin = cos_v[rows, lanes], sin_v[rows, lanes]
                out_v[0, rows, lanes] = re * cos - im * sin
                out_v[1, rows, lanes] = re * sin + im * cos
            return c

        lax.fori_loop(0, CPC, one, 0)
        copy = pltpu.make_async_copy(
            out_v.at[:, :, pl.ds(h * 512, 512)],
            out_hbm.at[:, :, pl.ds(h * 512, 512)],
            o_sem.at[h],
        )
        copy.start()
        return copy

    for h in range(HALVES):
        wait_bytes(r_in, rs_in, h, (DEVS - 1) * 32)
        transform(h)
        send_out(h)
    out_copies = []
    for h in range(HALVES):
        wait_bytes(r_out, rs_out, h, (DEVS - 1) * 16)
        out_copies.append(finish(h))
    for h in range(HALVES):
        wait_bytes(s_in, ss_in, h, (DEVS - 1) * 32)
        wait_bytes(s_out, ss_out, h, (DEVS - 1) * 16)
        out_copies[h].wait()


def local(hologram, phase, kept_blocks):
    g1, g2, tw = tables()
    f32, bf16 = jnp.float32, jnp.bfloat16
    hbm = pl.BlockSpec(memory_space=pl.ANY)
    pair = pltpu.SemaphoreType.DMA((HALVES,))
    return pl.pallas_call(
        kernel,
        out_shape=jax.ShapeDtypeStruct((2, 256, COLS), f32),
        in_specs=[hbm] * 5 + [pl.BlockSpec(memory_space=pltpu.SMEM)],
        out_specs=hbm,
        scratch_shapes=[
            pltpu.VMEM((HALVES, 2, ROWS, COLS // HALVES), f32),
            pltpu.VMEM((HALVES, DEVS * 32, 128), f32),
            pltpu.VMEM((HALVES, DEVS * 32, 128), f32),
            pltpu.VMEM((2 * 512, 8, 128), f32),
            pltpu.VMEM((HALVES, DEVS * 16, 128), f32),
            pltpu.VMEM((HALVES, DEVS * 16, 128), f32),
            pltpu.VMEM((256, COLS), f32),
            pltpu.VMEM((256, COLS), f32),
            pltpu.VMEM(g1.shape, bf16),
            pltpu.VMEM(g2.shape, bf16),
            pltpu.VMEM(tw.shape, f32),
            pltpu.VMEM((2, 256, COLS), f32),
            pair,
            pltpu.SemaphoreType.DMA((4,)),
            pair, pair, pair, pair, pair,
        ],
        compiler_params=pltpu.CompilerParams(
            collective_id=0, has_side_effects=True, vmem_limit_bytes=48 << 20
        ),
    )(hologram, phase, jnp.asarray(g1), jnp.asarray(g2), jnp.asarray(tw), kept_blocks)


def solution(mesh):
    in_specs = (P(None, "rows", None), P("rows", None), P())
    out_specs = P(None, "rows", None)
    return jax.shard_map(local, mesh=mesh, in_specs=in_specs, out_specs=out_specs, check_vma=False)
```

```python
import jax
import jax.numpy as jnp
import numpy as np
from jax import lax
from jax.experimental import pallas as pl
from jax.experimental.pallas import tpu as pltpu
from jax.sharding import PartitionSpec as P

MESH = pl.DeviceIdType.MESH
DEVS = 128
ROWS = 512
COLS = 1024
HALVES = 2
CPC = 4
RAD = 256
SPEC = 512 * 8
STEP = 37


def tables():
    def split(a):
        a = a.astype(np.float32)
        hi = a.astype(jnp.bfloat16)
        lo = (a - hi.astype(np.float32)).astype(jnp.bfloat16)
        return hi, lo

    def real_form(angle):
        cos, sin = np.cos(angle), np.sin(angle)
        return np.block([[cos, sin], [-sin, cos]])

    k = np.arange(RAD)
    m = np.concatenate([2 * np.arange(DEVS), 2 * np.arange(DEVS) + 1])
    first = real_form(2 * np.pi * (np.outer(k, m) % RAD) / RAD)
    second = real_form(2 * np.pi * (np.outer(k, k) % RAD) / RAD)
    out = []
    for mat in (first, second):
        hi, lo = split(mat)
        out.append(np.concatenate([hi, hi, lo], axis=1))
    angle = 2 * np.pi * np.outer(k, k) / (RAD * RAD)
    twiddle = np.stack([np.cos(angle), np.sin(angle)]) / RAD
    return out[0], out[1], twiddle.astype(np.float32)


def shifted(me, dy, dx, dz, dc):
    core = lax.rem(me + dc, 2)
    z = lax.rem(lax.div(me, 2) + dz, 4)
    x = lax.rem(lax.div(me, 8) + dx, 4)
    y = lax.rem(lax.div(me, 32) + dy, 4)
    return ((y * 4 + x) * 4 + z) * 2 + core


def peer_of(me, i):
    i = lax.rem(i * STEP, DEVS)
    return shifted(me, lax.div(i, 32), lax.div(i, 8), lax.div(i, 2), i)


def turn(axis, u, v, w):
    pick = lambda a, b, c: jnp.where(axis == 0, a, jnp.where(axis == 1, b, c))
    return pick(u, w, v), pick(v, u, w), pick(w, v, u)


def mate(me, i):
    j = lax.div(i, 2)
    far = 1 + lax.rem(lax.div(j, 3) + lax.rem(j, 3), 3)
    far = jnp.where(i == 18, 0, far)
    return shifted(me, *turn(lax.rem(j, 3), far, 0, 0), jnp.where(i == 18, 1, i))


def corner(me, i):
    j = lax.rem(i, 27)
    k = lax.div(j, 3)
    u = 1 + lax.rem(k, 3)
    v = 1 + lax.rem(lax.div(k, 3) + k, 3)
    return shifted(me, *turn(lax.rem(j, 3), u, v, 0), lax.div(i, 27))


def opposite(me, i):
    j = lax.rem(i, 27)
    k = lax.div(j, 3)
    u = lax.rem(j, 3)
    v = lax.rem(u + k, 3)
    w = lax.rem(u + 2 * k + lax.div(k, 3), 3)
    return shifted(me, 1 + u, 1 + v, 1 + w, lax.div(i, 27))


def split3(a, axis):
    hi = a.astype(jnp.bfloat16)
    lo = (a - hi.astype(jnp.float32)).astype(jnp.bfloat16)
    return jnp.concatenate([hi, lo, hi], axis=axis)


def aligned(v, m):
    return pl.multiple_of(v, m)


def kernel(
    x_hbm, phase_hbm, g1_hbm, g2_hbm, tw_hbm, kept, out_v,
    x_v, s_in, r_in, spec, s_out, r_out, cos_v, sin_v, g1, g2, tw,
    x_sem, t_sem, round2, round3, ss_in, rs_in, ss_out, rs_out,
):
    me = lax.axis_index("rows")
    barrier = pltpu.get_barrier_semaphore()

    def signal(sem, p):
        pl.semaphore_signal(sem, inc=1, device_id=(p,), device_id_type=MESH)

    def greet(i, c):
        signal(barrier, mate(me, i))
        return c

    lax.fori_loop(0, 19, greet, 0)

    x_copies = [
        pltpu.make_async_copy(
            x_hbm.at[:, :, pl.ds(h * 512, 512)], x_v.at[h], x_sem.at[h]
        )
        for h in range(HALVES)
    ]
    for copy in x_copies:
        copy.start()
    table_copies = [
        pltpu.make_async_copy(src, dst, t_sem.at[n])
        for n, (src, dst) in enumerate(
            [(phase_hbm, cos_v), (g1_hbm, g1), (g2_hbm, g2), (tw_hbm, tw)]
        )
    ]
    for copy in table_copies:
        copy.start()

    def prepare(h):
        x_copies[h].wait()
        for ri in range(2):

            def one(c4, c):
                block = x_v[h, ri, :, pl.ds(aligned(c4 * 128, 128), 128)].T
                for rq in range(4):
                    s_in[h, pl.ds(rq * 8 + ri * 4 + c4, DEVS, stride=32), :] = block[
                        :, rq * 128 : (rq + 1) * 128
                    ]
                return c

            lax.fori_loop(0, CPC, one, 0)

    def send_in(h, group, count):
        def one(i, c):
            p = group(me, i)
            pltpu.make_async_remote_copy(
                src_ref=s_in.at[h, pl.ds(aligned(p * 32, 32), 32)],
                dst_ref=r_in.at[h, pl.ds(aligned(me * 32, 32), 32)],
                send_sem=ss_in.at[h],
                recv_sem=rs_in.at[h],
                device_id=(p,),
                device_id_type=MESH,
            ).start()
            return c

        lax.fori_loop(0, count, one, 0)

    def keep_own(h):
        own = pl.ds(aligned(me * 32, 32), 32)
        r_in[h, own, :] = s_in[h, own, :]

    def wait_bytes(ref, sem, h, rows):
        part = ref.at[h, pl.ds(0, rows)]
        pltpu.make_async_copy(part, part, sem.at[h]).wait()

    prepare(0)
    pl.semaphore_wait(barrier, 19)
    for far in range(1, 4):
        signal(round2, shifted(me, 0, far, 0, 0))
        signal(round2, shifted(me, far, 0, 0, 0))
    send_in(0, mate, 19)
    pl.semaphore_wait(round2, 6)
    for far in range(1, 4):
        signal(round3, shifted(me, 0, far, 0, 0))
    send_in(0, corner, 54)
    prepare(1)
    send_in(1, mate, 19)
    pl.semaphore_wait(round3, 3)
    send_in(0, opposite, 54)
    send_in(1, corner, 54)
    send_in(1, opposite, 54)
    keep_own(0)
    keep_own(1)

    table_copies[0].wait()

    def trig(i, c):
        rows = pl.ds(aligned(i * 8, 8), 8)
        angle = cos_v[rows, :]
        cos_v[rows, :] = jnp.cos(angle)
        sin_v[rows, :] = jnp.sin(angle)
        return c

    lax.fori_loop(0, 32, trig, 0)
    for copy in table_copies[1:]:
        copy.wait()

    flat = spec.reshape(2 * SPEC, 128)

    def transform(h):
        def one(c4, c):
            parts = []
            for ri in range(2):
                for rh in range(2):
                    parts.append(
                        jnp.concatenate(
                            [
                                r_in[
                                    h,
                                    pl.ds(
                                        (rh * 2 + rl) * 8 + ri * 4 + c4,
                                        DEVS,
                                        stride=32,
                                    ),
                                    :,
                                ]
                                for rl in range(2)
                            ],
                            axis=1,
                        )
                    )
            a = split3(jnp.concatenate(parts, axis=0), 0)
            y = jnp.dot(g1[...], a, preferred_element_type=jnp.float32)
            y_re, y_im = y[:RAD], y[RAD:]
            t_re, t_im = tw[0], tw[1]
            b = jnp.concatenate(
                [y_re * t_re + y_im * t_im, y_im * t_re - y_re * t_im], axis=1
            )
            z = lax.dot_general(
                g2[...],
                split3(b, 1),
                (((1,), (1,)), ((), ())),
                preferred_element_type=jnp.float32,
            )
            for ro in range(2):
                for kh in range(2):
                    tile = z[ro * RAD : (ro + 1) * RAD, kh * 128 : (kh + 1) * 128]
                    swapped = jnp.concatenate([tile[:, 64:], tile[:, :64]], axis=1)
                    row = kh * 8 + ro * 4 + c4
                    flat[pl.ds(row, RAD, stride=16), :] = tile
                    flat[pl.ds(SPEC + row, RAD, stride=16), :] = swapped
            return c

        lax.fori_loop(0, CPC, one, 0)

    low = lax.broadcasted_iota(jnp.int32, (8, 128), 1) < 64

    def gather(p):
        tiles = []
        for jp in range(2):
            halves = []
            for par in range(2):
                b = kept[p * 4 + jp * 2 + par]
                halves.append(spec[lax.div(b, 2) + lax.rem(b + par, 2) * 512])
            tiles.append(jnp.where(low, halves[0], halves[1]))
        return jnp.concatenate(tiles, axis=0)

    def send_out(h):
        def one(i, c):
            p = peer_of(me, i)
            mine = pl.ds(aligned(p * 16, 16), 16)
            s_out[h, mine, :] = gather(p)
            pltpu.make_async_remote_copy(
                src_ref=s_out.at[h, mine],
                dst_ref=r_out.at[h, pl.ds(aligned(me * 16, 16), 16)],
                send_sem=ss_out.at[h],
                recv_sem=rs_out.at[h],
                device_id=(p,),
                device_id_type=MESH,
            ).start()
            return c

        lax.fori_loop(1, DEVS, one, 0)
        r_out[h, pl.ds(aligned(me * 16, 16), 16), :] = gather(me)

    def finish(h):
        def one(c4, c):
            lanes = pl.ds(aligned((h * CPC + c4) * 128, 128), 128)
            for jp in range(2):
                rows = pl.ds(jp * 128, 128)
                re, im = [
                    r_out[h, pl.ds(jp * 8 + ri * 4 + c4, DEVS, stride=16), :].T
                    for ri in range(2)
                ]
                cos, sin = cos_v[rows, lanes], sin_v[rows, lanes]
                out_v[0, rows, lanes] = re * cos - im * sin
                out_v[1, rows, lanes] = re * sin + im * cos
            return c

        lax.fori_loop(0, CPC, one, 0)

    for h in range(HALVES):
        wait_bytes(r_in, rs_in, h, (DEVS - 1) * 32)
        transform(h)
        send_out(h)
    for h in range(HALVES):
        wait_bytes(r_out, rs_out, h, (DEVS - 1) * 16)
        finish(h)
    for h in range(HALVES):
        wait_bytes(s_in, ss_in, h, (DEVS - 1) * 32)
        wait_bytes(s_out, ss_out, h, (DEVS - 1) * 16)


def local(hologram, phase, kept_blocks):
    g1, g2, tw = tables()
    f32, bf16 = jnp.float32, jnp.bfloat16
    hbm = pl.BlockSpec(memory_space=pl.ANY)
    pair = pltpu.SemaphoreType.DMA((HALVES,))
    return pl.pallas_call(
        kernel,
        out_shape=pltpu.VMEM((2, 256, COLS), f32),
        in_specs=[hbm] * 5 + [pl.BlockSpec(memory_space=pltpu.SMEM)],
        out_specs=pl.BlockSpec(memory_space=pltpu.VMEM),
        scratch_shapes=[
            pltpu.VMEM((HALVES, 2, ROWS, COLS // HALVES), f32),
            pltpu.VMEM((HALVES, DEVS * 32, 128), f32),
            pltpu.VMEM((HALVES, DEVS * 32, 128), f32),
            pltpu.VMEM((2 * 512, 8, 128), f32),
            pltpu.VMEM((HALVES, DEVS * 16, 128), f32),
            pltpu.VMEM((HALVES, DEVS * 16, 128), f32),
            pltpu.VMEM((256, COLS), f32),
            pltpu.VMEM((256, COLS), f32),
            pltpu.VMEM(g1.shape, bf16),
            pltpu.VMEM(g2.shape, bf16),
            pltpu.VMEM(tw.shape, f32),
            pair,
            pltpu.SemaphoreType.DMA((4,)),
            pltpu.SemaphoreType.REGULAR,
            pltpu.SemaphoreType.REGULAR,
            pair, pair, pair, pair,
        ],
        compiler_params=pltpu.CompilerParams(
            collective_id=0, has_side_effects=True, vmem_limit_bytes=61 << 20
        ),
    )(hologram, phase, jnp.asarray(g1), jnp.asarray(g2), jnp.asarray(tw), kept_blocks)


def solution(mesh):
    in_specs = (P(None, "rows", None), P("rows", None), P())
    out_specs = P(None, "rows", None)
    return jax.shard_map(local, mesh=mesh, in_specs=in_specs, out_specs=out_specs, check_vma=False)
```

```python
import jax
import jax.numpy as jnp
import numpy as np
from jax import lax
from jax.experimental import pallas as pl
from jax.experimental.pallas import tpu as pltpu
from jax.sharding import PartitionSpec as P

MESH = pl.DeviceIdType.MESH
DEVS = 128
ROWS = 512
COLS = 1024
HALVES = 2
CPC = 4
RAD = 256
SPEC = 512 * 8


def tables():
    def split(a):
        a = a.astype(np.float32)
        hi = a.astype(jnp.bfloat16)
        lo = (a - hi.astype(np.float32)).astype(jnp.bfloat16)
        return hi, lo

    def real_form(angle):
        cos, sin = np.cos(angle), np.sin(angle)
        return np.block([[cos, sin], [-sin, cos]])

    k = np.arange(RAD)
    m = np.concatenate([2 * np.arange(DEVS), 2 * np.arange(DEVS) + 1])
    first = real_form(2 * np.pi * (np.outer(k, m) % RAD) / RAD)
    second = real_form(2 * np.pi * (np.outer(k, k) % RAD) / RAD)
    out = []
    for mat in (first, second):
        hi, lo = split(mat)
        out.append(np.concatenate([hi, hi, lo], axis=1))
    angle = 2 * np.pi * np.outer(k, k) / (RAD * RAD)
    twiddle = np.stack([np.cos(angle), np.sin(angle)]) / RAD
    return out[0], out[1], twiddle.astype(np.float32)


def shifts():
    near = [(0, 0, 0, 1)]
    near += [
        tuple(far if a == axis else 0 for a in range(3)) + (core,)
        for far in (1, 3, 2)
        for axis in range(3)
        for core in range(2)
    ]
    corner, opposite = [], []
    for core in range(2):
        for k in range(9):
            u, v = 1 + k % 3, 1 + (k // 3 + k) % 3
            corner += [(u, v, 0, core), (0, u, v, core), (v, 0, u, core)]
        for j in range(27):
            k, u = divmod(j, 3)
            v, w = (u + k) % 3, (u + 2 * k + k // 3) % 3
            opposite.append((1 + u, 1 + v, 1 + w, core))
    return near + corner + opposite


SHIFTS = shifts()
MATES, CORNERS = 19, 54


def split3(a, axis):
    hi = a.astype(jnp.bfloat16)
    lo = (a - hi.astype(jnp.float32)).astype(jnp.bfloat16)
    return jnp.concatenate([hi, lo, hi], axis=axis)


def aligned(v, m):
    return pl.multiple_of(v, m)


def kernel(
    x_hbm, phase_hbm, g1_hbm, g2_hbm, tw_hbm, kept, out_v,
    peer, x_v, s_in, r_in, spec, s_out, r_out, cos_v, sin_v, g1, g2, tw,
    x_sem, t_sem, round2, round3, ss_in, rs_in, ss_out, rs_out,
):
    me = lax.axis_index("rows")
    barrier = pltpu.get_barrier_semaphore()

    def signal(sem, p):
        pl.semaphore_signal(sem, inc=1, device_id=(p,), device_id_type=MESH)

    place = [lax.rem(lax.div(me, w), n) for w, n in ((32, 4), (8, 4), (2, 4), (1, 2))]
    moved = [
        [lax.rem(v + d, n) * w for d in range(n)]
        for v, (w, n) in zip(place, ((32, 4), (8, 4), (2, 4), (1, 2)))
    ]

    def at(shift):
        y, x, z, core = [moved[axis][d] for axis, d in enumerate(shift)]
        return y + x + z + core

    for shift in SHIFTS[:MATES]:
        signal(barrier, at(shift))

    x_copies = [
        pltpu.make_async_copy(
            x_hbm.at[:, :, pl.ds(h * 512, 512)], x_v.at[h], x_sem.at[h]
        )
        for h in range(HALVES)
    ]
    for copy in x_copies:
        copy.start()
    table_copies = [
        pltpu.make_async_copy(src, dst, t_sem.at[n])
        for n, (src, dst) in enumerate(
            [(phase_hbm, cos_v), (g1_hbm, g1), (g2_hbm, g2), (tw_hbm, tw)]
        )
    ]
    for copy in table_copies:
        copy.start()

    def prepare(h):
        x_copies[h].wait()
        for ri in range(2):

            def one(c4, c):
                block = x_v[h, ri, :, pl.ds(aligned(c4 * 128, 128), 128)].T
                for rq in range(4):
                    s_in[h, pl.ds(rq * 8 + ri * 4 + c4, DEVS, stride=32), :] = block[
                        :, rq * 128 : (rq + 1) * 128
                    ]
                return c

            lax.fori_loop(0, CPC, one, 0)

    def send_in(h, first, last):
        def one(i, c):
            p = peer[i]
            pltpu.make_async_remote_copy(
                src_ref=s_in.at[h, pl.ds(aligned(p * 32, 32), 32)],
                dst_ref=r_in.at[h, pl.ds(aligned(me * 32, 32), 32)],
                send_sem=ss_in.at[h],
                recv_sem=rs_in.at[h],
                device_id=(p,),
                device_id_type=MESH,
            ).start()
            return c

        lax.fori_loop(first, last, one, 0)

    def keep_own(h):
        own = pl.ds(aligned(me * 32, 32), 32)
        r_in[h, own, :] = s_in[h, own, :]

    def wait_bytes(ref, sem, h, rows):
        part = ref.at[h, pl.ds(0, rows)]
        pltpu.make_async_copy(part, part, sem.at[h]).wait()

    for i, shift in enumerate(SHIFTS):
        peer[i] = at(shift)
    prepare(0)
    edge = MATES + CORNERS
    pl.semaphore_wait(barrier, MATES)
    for far in range(1, 4):
        signal(round2, at((0, far, 0, 0)))
        signal(round2, at((far, 0, 0, 0)))
    send_in(0, 0, MATES)
    prepare(1)
    pl.semaphore_wait(round2, 6)
    for far in range(1, 4):
        signal(round3, at((0, far, 0, 0)))
    send_in(0, MATES, edge)
    send_in(1, 0, MATES)
    pl.semaphore_wait(round3, 3)
    send_in(0, edge, DEVS - 1)
    send_in(1, MATES, edge)
    send_in(1, edge, DEVS - 1)
    keep_own(0)
    keep_own(1)

    table_copies[0].wait()

    def trig(i, c):
        rows = pl.ds(aligned(i * 8, 8), 8)
        angle = cos_v[rows, :]
        cos_v[rows, :] = jnp.cos(angle)
        sin_v[rows, :] = jnp.sin(angle)
        return c

    lax.fori_loop(0, 32, trig, 0)
    for copy in table_copies[1:]:
        copy.wait()

    flat = spec.reshape(2 * SPEC, 128)

    def transform(h):
        def one(c4, c):
            parts = []
            for ri in range(2):
                for rh in range(2):
                    parts.append(
                        jnp.concatenate(
                            [
                                r_in[
                                    h,
                                    pl.ds(
                                        (rh * 2 + rl) * 8 + ri * 4 + c4,
                                        DEVS,
                                        stride=32,
                                    ),
                                    :,
                                ]
                                for rl in range(2)
                            ],
                            axis=1,
                        )
                    )
            a = split3(jnp.concatenate(parts, axis=0), 0)
            y = jnp.dot(g1[...], a, preferred_element_type=jnp.float32)
            y_re, y_im = y[:RAD], y[RAD:]
            t_re, t_im = tw[0], tw[1]
            b = jnp.concatenate(
                [y_re * t_re + y_im * t_im, y_im * t_re - y_re * t_im], axis=1
            )
            z = lax.dot_general(
                g2[...],
                split3(b, 1),
                (((1,), (1,)), ((), ())),
                preferred_element_type=jnp.float32,
            )
            for ro in range(2):
                for kh in range(2):
                    tile = z[ro * RAD : (ro + 1) * RAD, kh * 128 : (kh + 1) * 128]
                    swapped = jnp.concatenate([tile[:, 64:], tile[:, :64]], axis=1)
                    row = kh * 8 + ro * 4 + c4
                    flat[pl.ds(row, RAD, stride=16), :] = tile
                    flat[pl.ds(SPEC + row, RAD, stride=16), :] = swapped
            return c

        lax.fori_loop(0, CPC, one, 0, unroll=4)

    low = lax.broadcasted_iota(jnp.int32, (8, 128), 1) < 64

    def gather(p):
        tiles = []
        for jp in range(2):
            halves = []
            for par in range(2):
                b = kept[p * 4 + jp * 2 + par]
                halves.append(spec[lax.div(b, 2) + lax.rem(b + par, 2) * 512])
            tiles.append(jnp.where(low, halves[0], halves[1]))
        return jnp.concatenate(tiles, axis=0)

    def send_out(h):
        def one(i, c):
            p = peer[DEVS - 1 - i]
            mine = pl.ds(aligned(p * 16, 16), 16)
            s_out[h, mine, :] = gather(p)
            pltpu.make_async_remote_copy(
                src_ref=s_out.at[h, mine],
                dst_ref=r_out.at[h, pl.ds(aligned(me * 16, 16), 16)],
                send_sem=ss_out.at[h],
                recv_sem=rs_out.at[h],
                device_id=(p,),
                device_id_type=MESH,
            ).start()
            return c

        lax.fori_loop(1, DEVS, one, 0, unroll=4)
        r_out[h, pl.ds(aligned(me * 16, 16), 16), :] = gather(me)

    def finish(h):
        def one(c4, c):
            lanes = pl.ds(aligned((h * CPC + c4) * 128, 128), 128)
            for jp in range(2):
                rows = pl.ds(jp * 128, 128)
                re, im = [
                    r_out[h, pl.ds(jp * 8 + ri * 4 + c4, DEVS, stride=16), :].T
                    for ri in range(2)
                ]
                cos, sin = cos_v[rows, lanes], sin_v[rows, lanes]
                out_v[0, rows, lanes] = re * cos - im * sin
                out_v[1, rows, lanes] = re * sin + im * cos
            return c

        lax.fori_loop(0, CPC, one, 0, unroll=4)

    for h in range(HALVES):
        wait_bytes(r_in, rs_in, h, (DEVS - 1) * 32)
        transform(h)
        send_out(h)
    for h in range(HALVES):
        wait_bytes(r_out, rs_out, h, (DEVS - 1) * 16)
        finish(h)
    for h in range(HALVES):
        wait_bytes(s_in, ss_in, h, (DEVS - 1) * 32)
        wait_bytes(s_out, ss_out, h, (DEVS - 1) * 16)


def local(hologram, phase, kept_blocks):
    g1, g2, tw = tables()
    f32, bf16 = jnp.float32, jnp.bfloat16
    hbm = pl.BlockSpec(memory_space=pl.ANY)
    pair = pltpu.SemaphoreType.DMA((HALVES,))
    return pl.pallas_call(
        kernel,
        out_shape=pltpu.VMEM((2, 256, COLS), f32),
        in_specs=[hbm] * 5 + [pl.BlockSpec(memory_space=pltpu.SMEM)],
        out_specs=pl.BlockSpec(memory_space=pltpu.VMEM),
        scratch_shapes=[
            pltpu.SMEM((DEVS,), jnp.int32),
            pltpu.VMEM((HALVES, 2, ROWS, COLS // HALVES), f32),
            pltpu.VMEM((HALVES, DEVS * 32, 128), f32),
            pltpu.VMEM((HALVES, DEVS * 32, 128), f32),
            pltpu.VMEM((2 * 512, 8, 128), f32),
            pltpu.VMEM((HALVES, DEVS * 16, 128), f32),
            pltpu.VMEM((HALVES, DEVS * 16, 128), f32),
            pltpu.VMEM((256, COLS), f32),
            pltpu.VMEM((256, COLS), f32),
            pltpu.VMEM(g1.shape, bf16),
            pltpu.VMEM(g2.shape, bf16),
            pltpu.VMEM(tw.shape, f32),
            pair,
            pltpu.SemaphoreType.DMA((4,)),
            pltpu.SemaphoreType.REGULAR,
            pltpu.SemaphoreType.REGULAR,
            pair, pair, pair, pair,
        ],
        compiler_params=pltpu.CompilerParams(
            collective_id=0, has_side_effects=True, vmem_limit_bytes=61 << 20
        ),
    )(hologram, phase, jnp.asarray(g1), jnp.asarray(g2), jnp.asarray(tw), kept_blocks)


def solution(mesh):
    in_specs = (P(None, "rows", None), P("rows", None), P())
    out_specs = P(None, "rows", None)
    return jax.shard_map(local, mesh=mesh, in_specs=in_specs, out_specs=out_specs, check_vma=False)
```

```python
import jax
import jax.numpy as jnp
import numpy as np
from jax import lax
from jax.experimental import pallas as pl
from jax.experimental.pallas import tpu as pltpu
from jax.sharding import PartitionSpec as P

MESH = pl.DeviceIdType.MESH
DEVS = 128
ROWS = 512
COLS = 1024
HALVES = 2
CPC = 4
RAD = 256
SPEC = 512 * 8


def tables():
    def split(a):
        a = a.astype(np.float32)
        hi = a.astype(jnp.bfloat16)
        lo = (a - hi.astype(np.float32)).astype(jnp.bfloat16)
        return hi, lo

    def real_form(angle):
        cos, sin = np.cos(angle), np.sin(angle)
        return np.block([[cos, sin], [-sin, cos]])

    k = np.arange(RAD)
    m = np.concatenate([2 * np.arange(DEVS), 2 * np.arange(DEVS) + 1])
    first = real_form(2 * np.pi * (np.outer(k, m) % RAD) / RAD)
    second = real_form(2 * np.pi * (np.outer(k, k) % RAD) / RAD)
    out = []
    for mat in (first, second):
        hi, lo = split(mat)
        out.append(np.concatenate([hi, hi, lo], axis=1))
    angle = 2 * np.pi * np.outer(k, k) / (RAD * RAD)
    twiddle = np.stack([np.cos(angle), np.sin(angle)]) / RAD
    return out[0], out[1], twiddle.astype(np.float32)


def shifts():
    near = [(0, 0, 0, 1)]
    near += [
        tuple(far if a == axis else 0 for a in range(3)) + (core,)
        for far in (1, 3, 2)
        for axis in range(3)
        for core in range(2)
    ]
    corner, opposite = [], []
    for core in range(2):
        for k in range(9):
            u, v = 1 + k % 3, 1 + (k // 3 + k) % 3
            corner += [(u, v, 0, core), (0, u, v, core), (v, 0, u, core)]
        for j in range(27):
            k, u = divmod(j, 3)
            v, w = (u + k) % 3, (u + 2 * k + k // 3) % 3
            opposite.append((1 + u, 1 + v, 1 + w, core))
    return near + corner + opposite


SHIFTS = shifts()
MATES, CORNERS = 19, 54


def split3(a, axis):
    hi = a.astype(jnp.bfloat16)
    lo = (a - hi.astype(jnp.float32)).astype(jnp.bfloat16)
    return jnp.concatenate([hi, lo, hi], axis=axis)


def aligned(v, m):
    return pl.multiple_of(v, m)


def kernel(
    x_hbm, phase_hbm, g1_hbm, g2_hbm, tw_hbm, kept, out_v,
    peer, x_v, s_in, r_in, spec, s_out, r_out, cos_v, sin_v, g1, g2, tw,
    x_sem, t_sem, round2, round3, ss_in, rs_in, ss_out, rs_out,
):
    me = lax.axis_index("rows")
    barrier = pltpu.get_barrier_semaphore()

    def signal(sem, p):
        pl.semaphore_signal(sem, inc=1, device_id=(p,), device_id_type=MESH)

    place = [lax.rem(lax.div(me, w), n) for w, n in ((32, 4), (8, 4), (2, 4), (1, 2))]
    moved = [
        [lax.rem(v + d, n) * w for d in range(n)]
        for v, (w, n) in zip(place, ((32, 4), (8, 4), (2, 4), (1, 2)))
    ]

    def at(shift):
        y, x, z, core = [moved[axis][d] for axis, d in enumerate(shift)]
        return y + x + z + core

    for shift in SHIFTS[:MATES]:
        signal(barrier, at(shift))

    x_copies = [
        pltpu.make_async_copy(
            x_hbm.at[:, :, pl.ds(h * 512, 512)], x_v.at[h], x_sem.at[h]
        )
        for h in range(HALVES)
    ]
    for copy in x_copies:
        copy.start()
    table_copies = [
        pltpu.make_async_copy(src, dst, t_sem.at[n])
        for n, (src, dst) in enumerate(
            [(phase_hbm, cos_v), (g1_hbm, g1), (g2_hbm, g2), (tw_hbm, tw)]
        )
    ]
    for copy in table_copies:
        copy.start()

    def prepare(h):
        x_copies[h].wait()
        for ri in range(2):

            def one(c4, c):
                block = x_v[h, ri, :, pl.ds(aligned(c4 * 128, 128), 128)].T
                for rq in range(4):
                    s_in[h, pl.ds(rq * 8 + ri * 4 + c4, DEVS, stride=32), :] = block[
                        :, rq * 128 : (rq + 1) * 128
                    ]
                return c

            lax.fori_loop(0, CPC, one, 0)

    def send_in(h, first, last):
        def one(i, c):
            p = peer[i]
            pltpu.make_async_remote_copy(
                src_ref=s_in.at[h, pl.ds(aligned(p * 32, 32), 32)],
                dst_ref=r_in.at[h, pl.ds(aligned(me * 32, 32), 32)],
                send_sem=ss_in.at[h],
                recv_sem=rs_in.at[h],
                device_id=(p,),
                device_id_type=MESH,
            ).start()
            return c

        lax.fori_loop(first, last, one, 0)

    def keep_own(h):
        own = pl.ds(aligned(me * 32, 32), 32)
        r_in[h, own, :] = s_in[h, own, :]

    def wait_bytes(ref, sem, h, rows):
        part = ref.at[h, pl.ds(0, rows)]
        pltpu.make_async_copy(part, part, sem.at[h]).wait()

    for i, shift in enumerate(SHIFTS):
        peer[i] = at(shift)
    prepare(0)
    edge = MATES + CORNERS
    pl.semaphore_wait(barrier, MATES)
    for far in range(1, 4):
        signal(round2, at((0, far, 0, 0)))
        signal(round2, at((far, 0, 0, 0)))
    send_in(0, 0, MATES)
    prepare(1)
    pl.semaphore_wait(round2, 6)
    for far in range(1, 4):
        signal(round3, at((0, far, 0, 0)))
    send_in(0, MATES, edge)
    send_in(1, 0, MATES)
    pl.semaphore_wait(round3, 3)
    send_in(0, edge, DEVS - 1)
    send_in(1, edge, DEVS - 1)
    send_in(1, MATES, edge)
    keep_own(0)
    keep_own(1)

    table_copies[0].wait()

    def trig(i, c):
        rows = pl.ds(aligned(i * 8, 8), 8)
        angle = cos_v[rows, :]
        cos_v[rows, :] = jnp.cos(angle)
        sin_v[rows, :] = jnp.sin(angle)
        return c

    lax.fori_loop(0, 32, trig, 0)
    for copy in table_copies[1:]:
        copy.wait()

    flat = spec.reshape(2 * SPEC, 128)

    def transform(h):
        def one(c4, c):
            parts = []
            for ri in range(2):
                for rh in range(2):
                    parts.append(
                        jnp.concatenate(
                            [
                                r_in[
                                    h,
                                    pl.ds(
                                        (rh * 2 + rl) * 8 + ri * 4 + c4,
                                        DEVS,
                                        stride=32,
                                    ),
                                    :,
                                ]
                                for rl in range(2)
                            ],
                            axis=1,
                        )
                    )
            a = split3(jnp.concatenate(parts, axis=0), 0)
            y = jnp.dot(g1[...], a, preferred_element_type=jnp.float32)
            y_re, y_im = y[:RAD], y[RAD:]
            t_re, t_im = tw[0], tw[1]
            b = jnp.concatenate(
                [y_re * t_re + y_im * t_im, y_im * t_re - y_re * t_im], axis=1
            )
            z = lax.dot_general(
                g2[...],
                split3(b, 1),
                (((1,), (1,)), ((), ())),
                preferred_element_type=jnp.float32,
            )
            for ro in range(2):
                for kh in range(2):
                    tile = z[ro * RAD : (ro + 1) * RAD, kh * 128 : (kh + 1) * 128]
                    swapped = jnp.concatenate([tile[:, 64:], tile[:, :64]], axis=1)
                    row = kh * 8 + ro * 4 + c4
                    flat[pl.ds(row, RAD, stride=16), :] = tile
                    flat[pl.ds(SPEC + row, RAD, stride=16), :] = swapped
            return c

        lax.fori_loop(0, CPC, one, 0, unroll=4)

    low = lax.broadcasted_iota(jnp.int32, (8, 128), 1) < 64

    def gather(p):
        tiles = []
        for jp in range(2):
            halves = []
            for par in range(2):
                b = kept[p * 4 + jp * 2 + par]
                halves.append(spec[lax.div(b, 2) + lax.rem(b + par, 2) * 512])
            tiles.append(jnp.where(low, halves[0], halves[1]))
        return jnp.concatenate(tiles, axis=0)

    def send_out(h):
        def one(i, c):
            p = peer[DEVS - 1 - i]
            mine = pl.ds(aligned(p * 16, 16), 16)
            s_out[h, mine, :] = gather(p)
            pltpu.make_async_remote_copy(
                src_ref=s_out.at[h, mine],
                dst_ref=r_out.at[h, pl.ds(aligned(me * 16, 16), 16)],
                send_sem=ss_out.at[h],
                recv_sem=rs_out.at[h],
                device_id=(p,),
                device_id_type=MESH,
            ).start()
            return c

        lax.fori_loop(1, DEVS, one, 0, unroll=4)
        r_out[h, pl.ds(aligned(me * 16, 16), 16), :] = gather(me)

    def finish(h):
        def one(c4, c):
            lanes = pl.ds(aligned((h * CPC + c4) * 128, 128), 128)
            for jp in range(2):
                rows = pl.ds(jp * 128, 128)
                re, im = [
                    r_out[h, pl.ds(jp * 8 + ri * 4 + c4, DEVS, stride=16), :].T
                    for ri in range(2)
                ]
                cos, sin = cos_v[rows, lanes], sin_v[rows, lanes]
                out_v[0, rows, lanes] = re * cos - im * sin
                out_v[1, rows, lanes] = re * sin + im * cos
            return c

        lax.fori_loop(0, CPC, one, 0, unroll=4)

    for h in range(HALVES):
        wait_bytes(r_in, rs_in, h, (DEVS - 1) * 32)
        transform(h)
        send_out(h)
    for h in range(HALVES):
        wait_bytes(r_out, rs_out, h, (DEVS - 1) * 16)
        finish(h)
    for h in range(HALVES):
        wait_bytes(s_in, ss_in, h, (DEVS - 1) * 32)
        wait_bytes(s_out, ss_out, h, (DEVS - 1) * 16)


def local(hologram, phase, kept_blocks):
    g1, g2, tw = tables()
    f32, bf16 = jnp.float32, jnp.bfloat16
    hbm = pl.BlockSpec(memory_space=pl.ANY)
    pair = pltpu.SemaphoreType.DMA((HALVES,))
    return pl.pallas_call(
        kernel,
        out_shape=pltpu.VMEM((2, 256, COLS), f32),
        in_specs=[hbm] * 5 + [pl.BlockSpec(memory_space=pltpu.SMEM)],
        out_specs=pl.BlockSpec(memory_space=pltpu.VMEM),
        scratch_shapes=[
            pltpu.SMEM((DEVS,), jnp.int32),
            pltpu.VMEM((HALVES, 2, ROWS, COLS // HALVES), f32),
            pltpu.VMEM((HALVES, DEVS * 32, 128), f32),
            pltpu.VMEM((HALVES, DEVS * 32, 128), f32),
            pltpu.VMEM((2 * 512, 8, 128), f32),
            pltpu.VMEM((HALVES, DEVS * 16, 128), f32),
            pltpu.VMEM((HALVES, DEVS * 16, 128), f32),
            pltpu.VMEM((256, COLS), f32),
            pltpu.VMEM((256, COLS), f32),
            pltpu.VMEM(g1.shape, bf16),
            pltpu.VMEM(g2.shape, bf16),
            pltpu.VMEM(tw.shape, f32),
            pair,
            pltpu.SemaphoreType.DMA((4,)),
            pltpu.SemaphoreType.REGULAR,
            pltpu.SemaphoreType.REGULAR,
            pair, pair, pair, pair,
        ],
        compiler_params=pltpu.CompilerParams(
            collective_id=0, has_side_effects=True, vmem_limit_bytes=61 << 20
        ),
    )(hologram, phase, jnp.asarray(g1), jnp.asarray(g2), jnp.asarray(tw), kept_blocks)


def solution(mesh):
    in_specs = (P(None, "rows", None), P("rows", None), P())
    out_specs = P(None, "rows", None)
    return jax.shard_map(local, mesh=mesh, in_specs=in_specs, out_specs=out_specs, check_vma=False)
```

```python
import jax
import jax.numpy as jnp
import numpy as np
from jax import lax
from jax.experimental import pallas as pl
from jax.experimental.pallas import tpu as pltpu
from jax.sharding import PartitionSpec as P

MESH = pl.DeviceIdType.MESH
DEVS = 128
ROWS = 512
COLS = 1024
HALVES = 2
CPC = 4
RAD = 256
SPEC = 512 * 8


def tables():
    def split(a):
        a = a.astype(np.float32)
        hi = a.astype(jnp.bfloat16)
        lo = (a - hi.astype(np.float32)).astype(jnp.bfloat16)
        return hi, lo

    def real_form(angle):
        cos, sin = np.cos(angle), np.sin(angle)
        return np.block([[cos, sin], [-sin, cos]])

    k = np.arange(RAD)
    m = np.concatenate([2 * np.arange(DEVS), 2 * np.arange(DEVS) + 1])
    first = real_form(2 * np.pi * (np.outer(k, m) % RAD) / RAD)
    second = real_form(2 * np.pi * (np.outer(k, k) % RAD) / RAD)
    out = []
    for mat in (first, second):
        hi, lo = split(mat)
        out.append(np.concatenate([hi, hi, lo], axis=1))
    angle = 2 * np.pi * np.outer(k, k) / (RAD * RAD)
    twiddle = np.stack([np.cos(angle), np.sin(angle)]) / RAD
    return out[0], out[1], twiddle.astype(np.float32)


def shifts():
    near = [(0, 0, 0, 1)]
    near += [
        tuple(far if a == axis else 0 for a in range(3)) + (core,)
        for far in (1, 3, 2)
        for axis in range(3)
        for core in range(2)
    ]
    corner, opposite = [], []
    for core in range(2):
        for k in range(9):
            u, v = 1 + k % 3, 1 + (k // 3 + k) % 3
            corner += [(u, v, 0, core), (0, u, v, core), (v, 0, u, core)]
        for j in range(27):
            k, u = divmod(j, 3)
            v, w = (u + k) % 3, (u + 2 * k + k // 3) % 3
            opposite.append((1 + u, 1 + v, 1 + w, core))
    return near + corner + opposite


SHIFTS = shifts()
MATES, CORNERS = 19, 54


def split3(a, axis):
    hi = a.astype(jnp.bfloat16)
    lo = (a - hi.astype(jnp.float32)).astype(jnp.bfloat16)
    return jnp.concatenate([hi, lo, hi], axis=axis)


def aligned(v, m):
    return pl.multiple_of(v, m)


def kernel(
    x_hbm, phase_hbm, g1_hbm, g2_hbm, tw_hbm, kept, out_v,
    peer, x_v, s_in, r_in, spec, s_out, r_out, cos_v, sin_v, g1, g2, tw,
    x_sem, t_sem, round2, round3, ss_in, rs_in, ss_out, rs_out,
):
    me = lax.axis_index("rows")
    barrier = pltpu.get_barrier_semaphore()

    def signal(sem, p):
        pl.semaphore_signal(sem, inc=1, device_id=(p,), device_id_type=MESH)

    place = [lax.rem(lax.div(me, w), n) for w, n in ((32, 4), (8, 4), (2, 4), (1, 2))]
    moved = [
        [lax.rem(v + d, n) * w for d in range(n)]
        for v, (w, n) in zip(place, ((32, 4), (8, 4), (2, 4), (1, 2)))
    ]

    def at(shift):
        y, x, z, core = [moved[axis][d] for axis, d in enumerate(shift)]
        return y + x + z + core

    for shift in SHIFTS[:MATES]:
        signal(barrier, at(shift))

    x_copies = [
        pltpu.make_async_copy(
            x_hbm.at[:, :, pl.ds(h * 512, 512)], x_v.at[h], x_sem.at[h]
        )
        for h in range(HALVES)
    ]
    for copy in x_copies:
        copy.start()
    table_copies = [
        pltpu.make_async_copy(src, dst, t_sem.at[n])
        for n, (src, dst) in enumerate(
            [(phase_hbm, cos_v), (g1_hbm, g1), (g2_hbm, g2), (tw_hbm, tw)]
        )
    ]
    for copy in table_copies:
        copy.start()

    def prepare(h):
        x_copies[h].wait()
        for ri in range(2):

            def one(c4, c):
                block = x_v[h, ri, :, pl.ds(aligned(c4 * 128, 128), 128)].T
                for rq in range(4):
                    s_in[h, pl.ds(rq * 8 + ri * 4 + c4, DEVS, stride=32), :] = block[
                        :, rq * 128 : (rq + 1) * 128
                    ]
                return c

            lax.fori_loop(0, CPC, one, 0)

    def send_in(h, first, last):
        def one(i, c):
            p = peer[i]
            pltpu.make_async_remote_copy(
                src_ref=s_in.at[h, pl.ds(aligned(p * 32, 32), 32)],
                dst_ref=r_in.at[h, pl.ds(aligned(me * 32, 32), 32)],
                send_sem=ss_in.at[h],
                recv_sem=rs_in.at[h],
                device_id=(p,),
                device_id_type=MESH,
            ).start()
            return c

        lax.fori_loop(first, last, one, 0)

    def keep_own(h):
        own = pl.ds(aligned(me * 32, 32), 32)
        r_in[h, own, :] = s_in[h, own, :]

    def wait_bytes(ref, sem, h, rows):
        part = ref.at[h, pl.ds(0, rows)]
        pltpu.make_async_copy(part, part, sem.at[h]).wait()

    for i, shift in enumerate(SHIFTS):
        peer[i] = at(shift)
    edge = MATES + CORNERS
    pl.semaphore_wait(barrier, MATES)
    for far in range(1, 4):
        signal(round2, at((0, far, 0, 0)))
        signal(round2, at((far, 0, 0, 0)))
    prepare(0)
    send_in(0, 0, MATES)
    pl.semaphore_wait(round2, 6)
    for far in range(1, 4):
        signal(round3, at((0, far, 0, 0)))
    send_in(0, MATES, edge)
    prepare(1)
    send_in(1, 0, MATES)
    pl.semaphore_wait(round3, 3)
    send_in(0, edge, DEVS - 1)
    send_in(1, edge, DEVS - 1)
    send_in(1, MATES, edge)
    keep_own(0)
    keep_own(1)

    table_copies[0].wait()

    def trig(i, c):
        rows = pl.ds(aligned(i * 8, 8), 8)
        angle = cos_v[rows, :]
        cos_v[rows, :] = jnp.cos(angle)
        sin_v[rows, :] = jnp.sin(angle)
        return c

    lax.fori_loop(0, 32, trig, 0)
    for copy in table_copies[1:]:
        copy.wait()

    flat = spec.reshape(2 * SPEC, 128)

    def transform(h):
        def one(c4, c):
            parts = []
            for ri in range(2):
                for rh in range(2):
                    parts.append(
                        jnp.concatenate(
                            [
                                r_in[
                                    h,
                                    pl.ds(
                                        (rh * 2 + rl) * 8 + ri * 4 + c4,
                                        DEVS,
                                        stride=32,
                                    ),
                                    :,
                                ]
                                for rl in range(2)
                            ],
                            axis=1,
                        )
                    )
            a = split3(jnp.concatenate(parts, axis=0), 0)
            y = jnp.dot(g1[...], a, preferred_element_type=jnp.float32)
            y_re, y_im = y[:RAD], y[RAD:]
            t_re, t_im = tw[0], tw[1]
            b = jnp.concatenate(
                [y_re * t_re + y_im * t_im, y_im * t_re - y_re * t_im], axis=1
            )
            z = lax.dot_general(
                g2[...],
                split3(b, 1),
                (((1,), (1,)), ((), ())),
                preferred_element_type=jnp.float32,
            )
            for ro in range(2):
                for kh in range(2):
                    tile = z[ro * RAD : (ro + 1) * RAD, kh * 128 : (kh + 1) * 128]
                    swapped = jnp.concatenate([tile[:, 64:], tile[:, :64]], axis=1)
                    row = kh * 8 + ro * 4 + c4
                    flat[pl.ds(row, RAD, stride=16), :] = tile
                    flat[pl.ds(SPEC + row, RAD, stride=16), :] = swapped
            return c

        lax.fori_loop(0, CPC, one, 0, unroll=4)

    low = lax.broadcasted_iota(jnp.int32, (8, 128), 1) < 64

    def gather(p):
        tiles = []
        for jp in range(2):
            halves = []
            for par in range(2):
                b = kept[p * 4 + jp * 2 + par]
                halves.append(spec[lax.div(b, 2) + lax.rem(b + par, 2) * 512])
            tiles.append(jnp.where(low, halves[0], halves[1]))
        return jnp.concatenate(tiles, axis=0)

    def send_out(h):
        def one(i, c):
            p = peer[lax.rem(edge + i - 1, DEVS - 1)]
            mine = pl.ds(aligned(p * 16, 16), 16)
            s_out[h, mine, :] = gather(p)
            pltpu.make_async_remote_copy(
                src_ref=s_out.at[h, mine],
                dst_ref=r_out.at[h, pl.ds(aligned(me * 16, 16), 16)],
                send_sem=ss_out.at[h],
                recv_sem=rs_out.at[h],
                device_id=(p,),
                device_id_type=MESH,
            ).start()
            return c

        lax.fori_loop(1, DEVS, one, 0, unroll=4)
        r_out[h, pl.ds(aligned(me * 16, 16), 16), :] = gather(me)

    def finish(h):
        def one(c4, c):
            lanes = pl.ds(aligned((h * CPC + c4) * 128, 128), 128)
            for jp in range(2):
                rows = pl.ds(jp * 128, 128)
                re, im = [
                    r_out[h, pl.ds(jp * 8 + ri * 4 + c4, DEVS, stride=16), :].T
                    for ri in range(2)
                ]
                cos, sin = cos_v[rows, lanes], sin_v[rows, lanes]
                out_v[0, rows, lanes] = re * cos - im * sin
                out_v[1, rows, lanes] = re * sin + im * cos
            return c

        lax.fori_loop(0, CPC, one, 0, unroll=4)

    for h in range(HALVES):
        wait_bytes(r_in, rs_in, h, (DEVS - 1) * 32)
        transform(h)
        send_out(h)
    for h in range(HALVES):
        wait_bytes(r_out, rs_out, h, (DEVS - 1) * 16)
        finish(h)
    for h in range(HALVES):
        wait_bytes(s_in, ss_in, h, (DEVS - 1) * 32)
        wait_bytes(s_out, ss_out, h, (DEVS - 1) * 16)


def local(hologram, phase, kept_blocks):
    g1, g2, tw = tables()
    f32, bf16 = jnp.float32, jnp.bfloat16
    hbm = pl.BlockSpec(memory_space=pl.ANY)
    pair = pltpu.SemaphoreType.DMA((HALVES,))
    return pl.pallas_call(
        kernel,
        out_shape=pltpu.VMEM((2, 256, COLS), f32),
        in_specs=[hbm] * 5 + [pl.BlockSpec(memory_space=pltpu.SMEM)],
        out_specs=pl.BlockSpec(memory_space=pltpu.VMEM),
        scratch_shapes=[
            pltpu.SMEM((DEVS,), jnp.int32),
            pltpu.VMEM((HALVES, 2, ROWS, COLS // HALVES), f32),
            pltpu.VMEM((HALVES, DEVS * 32, 128), f32),
            pltpu.VMEM((HALVES, DEVS * 32, 128), f32),
            pltpu.VMEM((2 * 512, 8, 128), f32),
            pltpu.VMEM((HALVES, DEVS * 16, 128), f32),
            pltpu.VMEM((HALVES, DEVS * 16, 128), f32),
            pltpu.VMEM((256, COLS), f32),
            pltpu.VMEM((256, COLS), f32),
            pltpu.VMEM(g1.shape, bf16),
            pltpu.VMEM(g2.shape, bf16),
            pltpu.VMEM(tw.shape, f32),
            pair,
            pltpu.SemaphoreType.DMA((4,)),
            pltpu.SemaphoreType.REGULAR,
            pltpu.SemaphoreType.REGULAR,
            pair, pair, pair, pair,
        ],
        compiler_params=pltpu.CompilerParams(
            collective_id=0, has_side_effects=True, vmem_limit_bytes=61 << 20
        ),
    )(hologram, phase, jnp.asarray(g1), jnp.asarray(g2), jnp.asarray(tw), kept_blocks)


def solution(mesh):
    in_specs = (P(None, "rows", None), P("rows", None), P())
    out_specs = P(None, "rows", None)
    return jax.shard_map(local, mesh=mesh, in_specs=in_specs, out_specs=out_specs, check_vma=False)
```

```python
import jax
import jax.numpy as jnp
import numpy as np
from jax import lax
from jax.experimental import pallas as pl
from jax.experimental.pallas import tpu as pltpu
from jax.sharding import PartitionSpec as P

MESH = pl.DeviceIdType.MESH
DEVS = 128
ROWS = 512
COLS = 1024
HALVES = 2
CPC = 4
RAD = 256
SPEC = 512 * 8


def tables():
    def split(a):
        a = a.astype(np.float32)
        hi = a.astype(jnp.bfloat16)
        lo = (a - hi.astype(np.float32)).astype(jnp.bfloat16)
        return hi, lo

    def real_form(angle):
        cos, sin = np.cos(angle), np.sin(angle)
        return np.block([[cos, sin], [-sin, cos]])

    k = np.arange(RAD)
    m = np.concatenate([2 * np.arange(DEVS), 2 * np.arange(DEVS) + 1])
    first = real_form(2 * np.pi * (np.outer(k, m) % RAD) / RAD)
    second = real_form(2 * np.pi * (np.outer(k, k) % RAD) / RAD)
    out = []
    for mat in (first, second):
        hi, lo = split(mat)
        out.append(np.concatenate([hi, hi, lo], axis=1))
    angle = 2 * np.pi * np.outer(k, k) / (RAD * RAD)
    twiddle = np.stack([np.cos(angle), np.sin(angle)]) / RAD
    return out[0], out[1], twiddle.astype(np.float32)


def shifts():
    near = [(0, 0, 0, 1)]
    near += [
        tuple(far if a == axis else 0 for a in range(3)) + (core,)
        for far in (1, 3, 2)
        for axis in range(3)
        for core in range(2)
    ]
    corner, opposite = [], []
    for core in range(2):
        for k in range(9):
            u, v = 1 + k % 3, 1 + (k // 3 + k) % 3
            corner += [(u, v, 0, core), (0, u, v, core), (v, 0, u, core)]
        for j in range(27):
            k, u = divmod(j, 3)
            v, w = (u + k) % 3, (u + 2 * k + k // 3) % 3
            opposite.append((1 + u, 1 + v, 1 + w, core))
    return near + corner + opposite


SHIFTS = shifts()
MATES, CORNERS = 19, 54


def split3(a, axis):
    hi = a.astype(jnp.bfloat16)
    lo = (a - hi.astype(jnp.float32)).astype(jnp.bfloat16)
    return jnp.concatenate([hi, lo, hi], axis=axis)


def aligned(v, m):
    return pl.multiple_of(v, m)


def kernel(
    x_hbm, phase_hbm, g1_hbm, g2_hbm, tw_hbm, kept, out_v,
    peer, x_v, s_in, r_in, spec, s_out, r_out, cos_v, sin_v, g1, g2, tw,
    x_sem, t_sem, round2, round3, ss_in, rs_in, ss_out, rs_out,
):
    me = lax.axis_index("rows")
    barrier = pltpu.get_barrier_semaphore()

    def signal(sem, p):
        pl.semaphore_signal(sem, inc=1, device_id=(p,), device_id_type=MESH)

    place = [lax.rem(lax.div(me, w), n) for w, n in ((32, 4), (8, 4), (2, 4), (1, 2))]
    moved = [
        [lax.rem(v + d, n) * w for d in range(n)]
        for v, (w, n) in zip(place, ((32, 4), (8, 4), (2, 4), (1, 2)))
    ]

    def at(shift):
        y, x, z, core = [moved[axis][d] for axis, d in enumerate(shift)]
        return y + x + z + core

    for shift in SHIFTS[:MATES]:
        signal(barrier, at(shift))

    x_copies = [
        [
            pltpu.make_async_copy(
                x_hbm.at[ri, :, pl.ds(h * 512, 512)], x_v.at[h, ri], x_sem.at[h, ri]
            )
            for ri in range(2)
        ]
        for h in range(HALVES)
    ]
    for copy in x_copies[0] + x_copies[1]:
        copy.start()
    table_copies = [
        pltpu.make_async_copy(src, dst, t_sem.at[n])
        for n, (src, dst) in enumerate(
            [(phase_hbm, cos_v), (g1_hbm, g1), (g2_hbm, g2), (tw_hbm, tw)]
        )
    ]
    for copy in table_copies:
        copy.start()

    def prepare(h):
        for ri in range(2):
            x_copies[h][ri].wait()

            def one(c4, c):
                block = x_v[h, ri, :, pl.ds(aligned(c4 * 128, 128), 128)].T
                for rq in range(4):
                    s_in[h, pl.ds(rq * 8 + ri * 4 + c4, DEVS, stride=32), :] = block[
                        :, rq * 128 : (rq + 1) * 128
                    ]
                return c

            lax.fori_loop(0, CPC, one, 0, unroll=2)

    def send_in(h, first, last):
        def one(i, c):
            p = peer[i]
            pltpu.make_async_remote_copy(
                src_ref=s_in.at[h, pl.ds(aligned(p * 32, 32), 32)],
                dst_ref=r_in.at[h, pl.ds(aligned(me * 32, 32), 32)],
                send_sem=ss_in.at[h],
                recv_sem=rs_in.at[h],
                device_id=(p,),
                device_id_type=MESH,
            ).start()
            return c

        lax.fori_loop(first, last, one, 0)

    def keep_own(h):
        own = pl.ds(aligned(me * 32, 32), 32)
        r_in[h, own, :] = s_in[h, own, :]

    def wait_bytes(ref, sem, h, rows):
        part = ref.at[h, pl.ds(0, rows)]
        pltpu.make_async_copy(part, part, sem.at[h]).wait()

    for i, shift in enumerate(SHIFTS):
        peer[i] = at(shift)
    edge = MATES + CORNERS
    pl.semaphore_wait(barrier, MATES)
    for far in range(1, 4):
        signal(round2, at((0, far, 0, 0)))
        signal(round2, at((far, 0, 0, 0)))
    prepare(0)
    send_in(0, 0, MATES)
    pl.semaphore_wait(round2, 6)
    for far in range(1, 4):
        signal(round3, at((0, far, 0, 0)))
    send_in(0, MATES, edge)
    prepare(1)
    send_in(1, 0, MATES)
    pl.semaphore_wait(round3, 3)
    send_in(0, edge, DEVS - 1)
    send_in(1, edge, DEVS - 1)
    send_in(1, MATES, edge)
    keep_own(0)
    keep_own(1)

    table_copies[0].wait()

    def trig(i, c):
        rows = pl.ds(aligned(i * 8, 8), 8)
        angle = cos_v[rows, :]
        cos_v[rows, :] = jnp.cos(angle)
        sin_v[rows, :] = jnp.sin(angle)
        return c

    lax.fori_loop(0, 32, trig, 0)
    for copy in table_copies[1:]:
        copy.wait()

    flat = spec.reshape(2 * SPEC, 128)

    def transform(h):
        def one(c4, c):
            parts = []
            for ri in range(2):
                for rh in range(2):
                    parts.append(
                        jnp.concatenate(
                            [
                                r_in[
                                    h,
                                    pl.ds(
                                        (rh * 2 + rl) * 8 + ri * 4 + c4,
                                        DEVS,
                                        stride=32,
                                    ),
                                    :,
                                ]
                                for rl in range(2)
                            ],
                            axis=1,
                        )
                    )
            a = split3(jnp.concatenate(parts, axis=0), 0)
            y = jnp.dot(g1[...], a, preferred_element_type=jnp.float32)
            y_re, y_im = y[:RAD], y[RAD:]
            t_re, t_im = tw[0], tw[1]
            b = jnp.concatenate(
                [y_re * t_re + y_im * t_im, y_im * t_re - y_re * t_im], axis=1
            )
            z = lax.dot_general(
                g2[...],
                split3(b, 1),
                (((1,), (1,)), ((), ())),
                preferred_element_type=jnp.float32,
            )
            for ro in range(2):
                for kh in range(2):
                    tile = z[ro * RAD : (ro + 1) * RAD, kh * 128 : (kh + 1) * 128]
                    swapped = jnp.concatenate([tile[:, 64:], tile[:, :64]], axis=1)
                    row = kh * 8 + ro * 4 + c4
                    flat[pl.ds(row, RAD, stride=16), :] = tile
                    flat[pl.ds(SPEC + row, RAD, stride=16), :] = swapped
            return c

        lax.fori_loop(0, CPC, one, 0, unroll=4)

    low = lax.broadcasted_iota(jnp.int32, (8, 128), 1) < 64

    def gather(p):
        tiles = []
        for jp in range(2):
            halves = []
            for par in range(2):
                b = kept[p * 4 + jp * 2 + par]
                halves.append(spec[lax.div(b, 2) + lax.rem(b + par, 2) * 512])
            tiles.append(jnp.where(low, halves[0], halves[1]))
        return jnp.concatenate(tiles, axis=0)

    def send_out(h):
        def one(i, c):
            p = peer[lax.rem(edge + i - 1, DEVS - 1)]
            mine = pl.ds(aligned(p * 16, 16), 16)
            s_out[h, mine, :] = gather(p)
            pltpu.make_async_remote_copy(
                src_ref=s_out.at[h, mine],
                dst_ref=r_out.at[h, pl.ds(aligned(me * 16, 16), 16)],
                send_sem=ss_out.at[h],
                recv_sem=rs_out.at[h],
                device_id=(p,),
                device_id_type=MESH,
            ).start()
            return c

        lax.fori_loop(1, DEVS, one, 0, unroll=4)
        r_out[h, pl.ds(aligned(me * 16, 16), 16), :] = gather(me)

    def finish(h):
        def one(c4, c):
            lanes = pl.ds(aligned((h * CPC + c4) * 128, 128), 128)
            for jp in range(2):
                rows = pl.ds(jp * 128, 128)
                re, im = [
                    r_out[h, pl.ds(jp * 8 + ri * 4 + c4, DEVS, stride=16), :].T
                    for ri in range(2)
                ]
                cos, sin = cos_v[rows, lanes], sin_v[rows, lanes]
                out_v[0, rows, lanes] = re * cos - im * sin
                out_v[1, rows, lanes] = re * sin + im * cos
            return c

        lax.fori_loop(0, CPC, one, 0, unroll=4)

    for h in range(HALVES):
        wait_bytes(r_in, rs_in, h, (DEVS - 1) * 32)
        transform(h)
        send_out(h)
    for h in range(HALVES):
        wait_bytes(r_out, rs_out, h, (DEVS - 1) * 16)
        finish(h)
    for h in range(HALVES):
        wait_bytes(s_in, ss_in, h, (DEVS - 1) * 32)
        wait_bytes(s_out, ss_out, h, (DEVS - 1) * 16)


def local(hologram, phase, kept_blocks):
    g1, g2, tw = tables()
    f32, bf16 = jnp.float32, jnp.bfloat16
    hbm = pl.BlockSpec(memory_space=pl.ANY)
    pair = pltpu.SemaphoreType.DMA((HALVES,))
    return pl.pallas_call(
        kernel,
        out_shape=pltpu.VMEM((2, 256, COLS), f32),
        in_specs=[hbm] * 5 + [pl.BlockSpec(memory_space=pltpu.SMEM)],
        out_specs=pl.BlockSpec(memory_space=pltpu.VMEM),
        scratch_shapes=[
            pltpu.SMEM((DEVS,), jnp.int32),
            pltpu.VMEM((HALVES, 2, ROWS, COLS // HALVES), f32),
            pltpu.VMEM((HALVES, DEVS * 32, 128), f32),
            pltpu.VMEM((HALVES, DEVS * 32, 128), f32),
            pltpu.VMEM((2 * 512, 8, 128), f32),
            pltpu.VMEM((HALVES, DEVS * 16, 128), f32),
            pltpu.VMEM((HALVES, DEVS * 16, 128), f32),
            pltpu.VMEM((256, COLS), f32),
            pltpu.VMEM((256, COLS), f32),
            pltpu.VMEM(g1.shape, bf16),
            pltpu.VMEM(g2.shape, bf16),
            pltpu.VMEM(tw.shape, f32),
            pltpu.SemaphoreType.DMA((HALVES, 2)),
            pltpu.SemaphoreType.DMA((4,)),
            pltpu.SemaphoreType.REGULAR,
            pltpu.SemaphoreType.REGULAR,
            pair, pair, pair, pair,
        ],
        compiler_params=pltpu.CompilerParams(
            collective_id=0, has_side_effects=True, vmem_limit_bytes=61 << 20
        ),
    )(hologram, phase, jnp.asarray(g1), jnp.asarray(g2), jnp.asarray(tw), kept_blocks)


def solution(mesh):
    in_specs = (P(None, "rows", None), P("rows", None), P())
    out_specs = P(None, "rows", None)
    return jax.shard_map(local, mesh=mesh, in_specs=in_specs, out_specs=out_specs, check_vma=False)
```
